32 devices in a mesh: groups: 2 (over y), dp: 8 (over z, x), tensor: 2 (over core).
Axes of the slice: x: 2, y: 2, z: 4, core: 2. Of those that a mesh axis runs over, the one named last changes fastest.
Arguments:
- tokens_in: bfloat16 [2048, 4096], P(('groups', 'dp'), 'tensor'), parts along dimension 0, may hold values from -6 to 6
- grads_out: bfloat16 [2048, 12288], P(('groups', 'dp'), 'tensor'), parts along dimension 0, may hold values from -6 to 6
- proj_in: bfloat16 [4096, 64], P('tensor'), may hold values from -0.09375 to 0.09375
- proj_out: bfloat16 [12288, 64], P('tensor'), may hold values from -0.0546875 to 0.0546875
- lengths: int32 [16, 32], P('groups'), parts along dimension 0, may hold values from 1 to 64, 128 in all within a row
- train_feats: bfloat16 [6144, 4096], P(('groups', 'dp'), 'tensor'), parts along dimension 0, may hold values from -0.09375 to 0.09375
Outputs:
- scores: bfloat16 [512, 3072], P(('groups', 'tensor'), 'dp'), parts along dimension 0
The draws below stay inside these ranges and needn't reach their ends.
There are 2 independent parts, one for each index of `groups`. The reference program is written for one: setup_inputs(seed, part) draws one part's arguments, and reference() takes and returns one part's arrays. A program takes and returns all parts, laid end to end along the dimension named above; an argument that names none is the same for every part. Nothing has to cross between parts.
Inputs may be any that keep to these rules, and one draw needn't show every extreme that they name: Each row of 32 lengths sums to 128, and some example in each row has exactly 64 tokens.
All inputs are finite; a program needn't handle non-finite values.
Results may differ from the reference program's by a relative error of at most 0.0049.
Values may be sent and summed in bfloat16 or wider, within the bound.
A program may use at most 128 MiB of HBM per device.

```python
import math
import jax
import jax.numpy as jnp
import numpy as np
from jax import lax

D = 4096
FF = 12288
K = 64
TOK_DEV = 128
EX_DEV = 32
MOST = 64
DP_BLOCKS = 8
TOKENS = 1024
TRAIN = 3072
FEAT = 4096
N_DP = 8


def block_levels(stream_key, dims, pieces, least, high):
    factor_of, own = 1.0, jax.random.fold_in(stream_key, 6)
    for dim, blocks in pieces:
        draws = jnp.exp(jax.random.uniform(jax.random.fold_in(own, dim), (blocks,), jnp.float32, least / len(pieces), high / len(pieces)))
        factor_of = factor_of * jnp.repeat(draws, dims[dim] // blocks).reshape([-1 if axis == dim else 1 for axis in range(len(dims))])
    return factor_of


def split_up(number_of, total, reach, lean):
    weights = [(1 << 20) // math.isqrt(rank ** lean) + 1 for rank in range(2, number_of + 1)]
    surplus, given = total - reach - (number_of - 1), [1] * (number_of - 1)
    while surplus > 0:
        movable = [i for i in range(number_of - 1) if given[i] < reach]
        whole, budget = sum([weights[i] for i in movable]), surplus
        for i in movable:
            addition = min(reach - given[i], max(1, budget * weights[i] // whole), surplus)
            given[i] = given[i] + addition
            surplus = surplus - addition
    return np.array([reach] + given)


def ragged_sizes(key, number_of, total, limit, slope):
    if number_of == 2:
        one = jax.random.randint(key, (), max(1, total - limit), min(limit, total - 1) + 1)
        return jnp.stack([one, total - one])
    sizes = jnp.asarray(split_up(number_of, total, limit, slope), jnp.int32)
    pairs = (number_of - 1) // 2
    source_of, sink = sizes[1:1 + 2 * pairs:2], sizes[2:2 + 2 * pairs:2]
    room = jnp.minimum(source_of - 1, limit - sink)
    passed = jax.random.randint(jax.random.fold_in(key, 1), (pairs,), 0, 1 << 20) % (room + 1)
    sizes = sizes.at[1:1 + 2 * pairs:2].set(source_of - passed).at[2:2 + 2 * pairs:2].set(sink + passed)
    return sizes[jax.random.permutation(jax.random.fold_in(key, 2), number_of)]


def gaussian(own_key, extent, width, reach, shards=(), kind=jnp.bfloat16):
    drawn = jax.random.normal(own_key, extent, jnp.float32) * width
    if len(shards) > 0:
        drawn = block_levels(own_key, extent, shards, -0.22, 0.18) * drawn
    return jnp.clip(drawn, min=-reach, max=reach).astype(kind)


def setup_inputs(seed: int = 0, part: int = 0) -> dict:
    streams_of = jax.random.split(jax.random.key(seed), 7)
    own_keys = jax.random.split(jax.random.fold_in(streams_of[6], part), 7)
    tokens_in = gaussian(own_keys[0], (TOKENS, D), 1.0, 6.0, ((0, 8), (1, 2)))
    grads_out = gaussian(own_keys[1], (TOKENS, FF), 1.0, 6.0, ((0, 8), (1, 2)))
    proj_in = gaussian(streams_of[2], (D, K), D ** -0.5, 0.09375, ((0, 2),))
    proj_out = gaussian(streams_of[3], (FF, K), FF ** -0.5, 0.0546875, ((0, 2),))
    lengths = jax.vmap(lambda own: ragged_sizes(own, EX_DEV, TOK_DEV, MOST, 1))(jax.random.split(own_keys[4], DP_BLOCKS)).reshape((DP_BLOCKS, EX_DEV)).astype(jnp.int32)
    train_feats = gaussian(own_keys[5], (TRAIN, FEAT), 0.015625, 0.09375, ((0, 8), (1, 2)))
    return dict(tokens_in=tokens_in, grads_out=grads_out, proj_in=proj_in, proj_out=proj_out, lengths=lengths, train_feats=train_feats)


def reference(tokens_in, grads_out, proj_in, proj_out, lengths, train_feats):
    x_proj = jnp.dot(tokens_in, proj_in, preferred_element_type=jnp.float32)
    g_proj = jnp.dot(grads_out, proj_out, preferred_element_type=jnp.float32)
    stop_at = jnp.cumsum(lengths, axis=1).astype(jnp.int32)
    start_at = (stop_at - lengths).astype(jnp.int32)
    position = jnp.arange(TOK_DEV, dtype=jnp.int32)
    member = ((position[None, None, :] >= start_at[:, :, None]) & (position[None, None, :] < stop_at[:, :, None])).astype(jnp.float32)
    x_blocks = x_proj.reshape(N_DP, TOK_DEV, K)
    g_blocks = g_proj.reshape(N_DP, TOK_DEV, K)
    outer_rows = (x_blocks[:, :, :, None] * g_blocks[:, :, None, :]).reshape(N_DP, TOK_DEV, K * K)
    features = jnp.einsum("net,ntf->nef", member, outer_rows, precision=lax.Precision.HIGHEST)
    query_feats = features.reshape(EX_DEV * N_DP, K * K).astype(jnp.bfloat16)
    totals = lax.dot_general(query_feats, train_feats, (((1,), (1,)), ((), ())), preferred_element_type=jnp.float32)
    return totals.astype(jnp.bfloat16)
```

```python
import functools

import jax
import jax.numpy as jnp
from jax import lax
from jax.experimental import pallas as pl
from jax.experimental.pallas import tpu as pltpu
from jax.sharding import PartitionSpec as P

G_PIECES = 2
GROUP = 4
F_PIECES = 8


def peer(**axes):
    return dict(device_id=axes, device_id_type=pl.DeviceIdType.MESH)


def nt(a, b):
    return lax.dot_general(a, b, (((1,), (1,)), ((), ())), preferred_element_type=jnp.float32)


def nn(a, b):
    return jnp.dot(a, b, preferred_element_type=jnp.float32)


def kernel(n_dp, tok_hbm, grd_hbm, pin_hbm, pout_hbm, len_hbm, train_hbm, out_ref,
           tok, grd, pin, pout, lens, train, part, other, xg, outer,
           load_sem, train_sem, swap_send, swap_recv, a_send, a_recv, b_send, b_recv):
    n_blocks = n_dp // 2
    group = min(GROUP, n_blocks)
    dp = lax.axis_index("dp")
    core = lax.axis_index("tensor")
    sibling = 1 - core
    owner = dp // n_blocks == core
    slot = lax.rem(dp, n_blocks)
    K, n_tok = part.shape[1:]
    n_ex = lens.shape[1]
    ff = grd.shape[1] // G_PIECES

    barrier = pltpu.get_barrier_semaphore()
    pl.semaphore_signal(barrier, inc=1, **peer(tensor=sibling))

    def greet(j, carry):
        to = core * n_blocks + j

        @pl.when(to != dp)
        def _():
            pl.semaphore_signal(barrier, inc=1, **peer(dp=to))

        return carry

    lax.fori_loop(0, n_blocks, greet, 0, unroll=n_blocks <= 8)

    loads = [
        pltpu.make_async_copy(pin_hbm, pin, load_sem.at[0]),
        pltpu.make_async_copy(tok_hbm, tok, load_sem.at[1]),
    ]
    for k in range(G_PIECES):
        cols = pl.ds(k * ff, ff)
        loads.append(pltpu.make_async_copy(pout_hbm.at[:, cols], pout.at[:, cols], load_sem.at[2 + 2 * k]))
        loads.append(pltpu.make_async_copy(grd_hbm.at[:, cols], grd.at[:, cols], load_sem.at[3 + 2 * k]))
    loads.append(pltpu.make_async_copy(len_hbm, lens, load_sem.at[2 + 2 * G_PIECES]))
    for load in loads:
        load.start()
    own_train = pltpu.make_async_copy(train_hbm, train.at[core], train_sem)
    own_train.start()

    @pl.when(owner)
    def _():
        pl.semaphore_wait(barrier, n_dp)

    @pl.when(jnp.logical_not(owner))
    def _():
        pl.semaphore_wait(barrier, 1)

    swap = pltpu.make_async_remote_copy(
        train_hbm, train.at[core], swap_send, swap_recv, **peer(tensor=sibling))
    swap.start()

    def to_owner(p):
        return pltpu.make_async_remote_copy(
            part.at[p], other.at[p], a_send.at[p], a_recv.at[p], **peer(tensor=sibling))

    def to_peer(p, k):
        return pltpu.make_async_remote_copy(
            xg.at[slot, p], xg.at[slot, p], b_send.at[p, k], b_recv.at[slot, p],
            **peer(dp=lax.rem(dp + k, n_dp)))

    def each_peer(act):
        def step(k, carry):
            act(k)
            return carry

        lax.fori_loop(1, n_dp, step, 0, unroll=n_dp <= 8)

    def hand_over(p):
        @pl.when(jnp.logical_not(owner))
        def _():
            to_owner(p).start()

    def spread(p):
        @pl.when(owner)
        def _():
            to_owner(p).wait_recv()
            xg[slot, p] = (part[p] + other[p]).astype(jnp.bfloat16)
            each_peer(lambda k: to_peer(p, k).start())

    loads[0].wait()
    loads[1].wait()
    part[0] = nt(pin[...], tok[...])
    hand_over(0)
    for k in range(G_PIECES):
        loads[2 + 2 * k].wait()
        loads[3 + 2 * k].wait()
        term = nt(pout[:, k * ff:(k + 1) * ff], grd[:, k * ff:(k + 1) * ff])
        if k == 0:
            part[1] = term
            spread(0)
        else:
            part[1] += term
    hand_over(1)
    spread(1)

    loads[-1].wait()
    q_all = group * n_ex
    k_of = lax.broadcasted_iota(jnp.int32, (n_ex, q_all), 0)
    e_of = lax.rem(lax.broadcasted_iota(jnp.int32, (n_ex, q_all), 1), n_ex)
    lens_f = lens[...].astype(jnp.float32).astype(jnp.bfloat16)
    stops = nn(lens_f, (k_of <= e_of).astype(jnp.float32).astype(jnp.bfloat16))
    starts = nn(lens_f, (k_of < e_of).astype(jnp.float32).astype(jnp.bfloat16))
    row_of = lax.broadcasted_iota(jnp.int32, (n_dp, q_all), 0)
    block_of = lax.broadcasted_iota(jnp.int32, (n_dp, q_all), 1) // n_ex
    t_of = lax.broadcasted_iota(jnp.int32, (group * n_tok, q_all), 0)
    q_of = lax.broadcasted_iota(jnp.int32, (group * n_tok, q_all), 1)
    same = t_of // n_tok == q_of // n_ex
    place = lax.rem(t_of, n_tok).astype(jnp.float32)

    def score(first, wait_train):
        mine = row_of == core * n_blocks + first + block_of
        stop = jnp.sum(jnp.where(mine, stops, 0.0), axis=0, keepdims=True)
        start = jnp.sum(jnp.where(mine, starts, 0.0), axis=0, keepdims=True)
        member = jnp.where(same & (place >= start) & (place < stop), 1.0, 0.0).astype(jnp.bfloat16)

        for j in range(group):
            at = first + j

            @pl.when(jnp.logical_not(owner & (at == slot)))
            def _():
                for p in range(2):
                    pltpu.make_async_remote_copy(
                        xg.at[at, p], xg.at[at, p], b_send.at[p, 0], b_recv.at[at, p],
                        **peer(tensor=sibling)).wait_recv()

            x = xg[at, 0].astype(jnp.float32)
            g = xg[at, 1]
            for i in range(K):
                row = jnp.broadcast_to(x[i:i + 1], (16, n_tok)).astype(jnp.bfloat16)
                outer[i * K:(i + 1) * K, j * n_tok:(j + 1) * n_tok] = (
                    jnp.concatenate([row] * (K // 16), axis=0) * g)

        wait_train()
        size = K * K // F_PIECES
        half = K * K // 2
        acc = None
        for c in range(F_PIECES):
            rows = slice(c * size, (c + 1) * size)
            f = nn(outer[rows, :], member).astype(jnp.bfloat16)
            h, at = divmod(c * size, half)
            term = nn(train[h, :, at:at + size], f)
            acc = term if acc is None else acc + term
        return acc.T.astype(out_ref.dtype)

    def train_here():
        own_train.wait()
        pltpu.make_async_remote_copy(
            train_hbm, train.at[sibling], swap_send, swap_recv, **peer(tensor=sibling)).wait_recv()

    if n_blocks == group:
        out_ref[...] = score(0, train_here)
    else:
        train_here()

        def step(s, carry):
            out_ref[pl.ds(pl.multiple_of(s * q_all, q_all), q_all), :] = score(s * group, lambda: None)
            return carry

        lax.fori_loop(0, n_blocks // group, step, 0)

    swap.wait_send()

    @pl.when(jnp.logical_not(owner))
    def _():
        for p in range(2):
            to_owner(p).wait_send()

    @pl.when(owner)
    def _():
        for p in range(2):
            each_peer(lambda k: to_peer(p, k).wait_send())


def shards(n_dp, tokens_in, grads_out, proj_in, proj_out, lengths, train_feats):
    n_tok, d = tokens_in.shape
    ff = grads_out.shape[1]
    K = proj_in.shape[1]
    n_ex = lengths.shape[1]
    n_train, half = train_feats.shape
    n_blocks = n_dp // 2
    group = min(GROUP, n_blocks)
    bf16, f32 = jnp.bfloat16, jnp.float32
    dma = pltpu.SemaphoreType.DMA
    return pl.pallas_call(
        functools.partial(kernel, n_dp),
        out_shape=jax.ShapeDtypeStruct((n_blocks * n_ex, n_train), bf16),
        in_specs=[pl.BlockSpec(memory_space=pltpu.HBM)] * 6,
        out_specs=pl.BlockSpec(memory_space=pltpu.VMEM),
        scratch_shapes=[
            pltpu.VMEM((n_tok, d), bf16),
            pltpu.VMEM((n_tok, ff), bf16),
            pltpu.VMEM((K, d), bf16),
            pltpu.VMEM((K, ff), bf16),
            pltpu.VMEM(lengths.shape, jnp.int32),
            pltpu.VMEM((2, n_train, half), bf16),
            pltpu.VMEM((2, K, n_tok), f32),
            pltpu.VMEM((2, K, n_tok), f32),
            pltpu.VMEM((n_blocks, 2, K, n_tok), bf16),
            pltpu.VMEM((K * K, group * n_tok), bf16),
            dma((3 + 2 * G_PIECES,)),
            dma,
            dma,
            dma,
            dma((2,)),
            dma((2,)),
            dma((2, n_dp)),
            dma((n_blocks, 2)),
        ],
        compiler_params=pltpu.CompilerParams(
            collective_id=0, has_side_effects=True, vmem_limit_bytes=63 * 1024 * 1024),
        cost_estimate=pl.CostEstimate(flops=10**9, bytes_accessed=5 * 10**6, transcendentals=0),
    )(tokens_in, grads_out, proj_in.T, proj_out.T, lengths, train_feats)


def solution(mesh):
    return jax.shard_map(
        functools.partial(shards, mesh.shape["dp"]),
        mesh=mesh,
        in_specs=(
            P(("groups", "dp"), "tensor"),
            P(("groups", "dp"), "tensor"),
            P("tensor", None),
            P("tensor", None),
            P("groups", None),
            P(("groups", "dp"), "tensor"),
        ),
        out_specs=P(("groups", "tensor"), "dp"),
        check_vma=False,
    )
```

```python
import functools

import jax
import jax.numpy as jnp
from jax import lax
from jax.experimental import pallas as pl
from jax.experimental.pallas import tpu as pltpu
from jax.sharding import PartitionSpec as P

G_PIECES = 2
GROUP = 4


def peer(**axes):
    return dict(device_id=axes, device_id_type=pl.DeviceIdType.MESH)


def nt(a, b):
    return lax.dot_general(a, b, (((1,), (1,)), ((), ())), preferred_element_type=jnp.float32)


def nn(a, b):
    return jnp.dot(a, b, preferred_element_type=jnp.float32)


def kernel(n_dp, tok_hbm, grd_hbm, pin_hbm, pout_hbm, len_hbm, train_hbm, out_ref,
           tok, grd, pin, pout, lens, train, part, other, xg, outer, feats,
           load_sem, train_sem, swap_send, swap_recv, a_send, a_recv, b_send, b_recv):
    n_blocks = n_dp // 2
    group = min(GROUP, n_blocks)
    dp = lax.axis_index("dp")
    core = lax.axis_index("tensor")
    sibling = 1 - core
    owner = dp // n_blocks == core
    slot = lax.rem(dp, n_blocks)
    K, n_tok = part.shape[1:]
    n_ex = lens.shape[1]
    ff = grd.shape[1] // G_PIECES

    barrier = pltpu.get_barrier_semaphore()
    pl.semaphore_signal(barrier, inc=1, **peer(tensor=sibling))

    def greet(j, carry):
        to = core * n_blocks + j

        @pl.when(to != dp)
        def _():
            pl.semaphore_signal(barrier, inc=1, **peer(dp=to))

        return carry

    lax.fori_loop(0, n_blocks, greet, 0, unroll=n_blocks <= 8)

    loads = [
        pltpu.make_async_copy(pin_hbm, pin, load_sem.at[0]),
        pltpu.make_async_copy(tok_hbm, tok, load_sem.at[1]),
    ]
    for k in range(G_PIECES):
        cols = pl.ds(k * ff, ff)
        loads.append(pltpu.make_async_copy(pout_hbm.at[:, cols], pout.at[:, cols], load_sem.at[2 + 2 * k]))
        loads.append(pltpu.make_async_copy(grd_hbm.at[:, cols], grd.at[:, cols], load_sem.at[3 + 2 * k]))
    loads.append(pltpu.make_async_copy(len_hbm, lens, load_sem.at[2 + 2 * G_PIECES]))
    for load in loads:
        load.start()
    own_train = pltpu.make_async_copy(train_hbm, train.at[core], train_sem)
    own_train.start()

    swap = pltpu.make_async_remote_copy(
        train_hbm, train.at[core], swap_send, swap_recv, **peer(tensor=sibling))

    def to_owner(p):
        return pltpu.make_async_remote_copy(
            part.at[p], other.at[p], a_send.at[p], a_recv.at[p], **peer(tensor=sibling))

    def to_peer(p, k):
        return pltpu.make_async_remote_copy(
            xg.at[slot, p], xg.at[slot, p], b_send.at[p, k], b_recv.at[slot, p],
            **peer(dp=lax.rem(dp + k, n_dp)))

    def each_peer(act):
        def step(k, carry):
            act(k)
            return carry

        lax.fori_loop(1, n_dp, step, 0, unroll=n_dp <= 8)

    def hand_over(p):
        @pl.when(jnp.logical_not(owner))
        def _():
            if p == 0:
                pl.semaphore_wait(barrier, 1)
            to_owner(p).start()

    def spread(p):
        @pl.when(owner)
        def _():
            to_owner(p).wait_recv()
            xg[slot, p] = (part[p] + other[p]).astype(jnp.bfloat16)
            if p == 0:
                pl.semaphore_wait(barrier, n_dp)
            each_peer(lambda k: to_peer(p, k).start())

    loads[0].wait()
    loads[1].wait()
    part[0] = nt(pin[...], tok[...])
    hand_over(0)
    for k in range(G_PIECES):
        loads[2 + 2 * k].wait()
        loads[3 + 2 * k].wait()
        term = nt(pout[:, k * ff:(k + 1) * ff], grd[:, k * ff:(k + 1) * ff])
        if k == 0:
            part[1] = term
        else:
            part[1] += term
    hand_over(1)
    spread(0)
    spread(1)
    swap.start()

    loads[-1].wait()
    q_all = group * n_ex
    k_of = lax.broadcasted_iota(jnp.int32, (n_ex, q_all), 0)
    e_of = lax.rem(lax.broadcasted_iota(jnp.int32, (n_ex, q_all), 1), n_ex)
    lens_f = lens[...].astype(jnp.float32).astype(jnp.bfloat16)
    stops = nn(lens_f, (k_of <= e_of).astype(jnp.float32).astype(jnp.bfloat16))
    starts = nn(lens_f, (k_of < e_of).astype(jnp.float32).astype(jnp.bfloat16))
    row_of = lax.broadcasted_iota(jnp.int32, (n_dp, q_all), 0)
    block_of = lax.broadcasted_iota(jnp.int32, (n_dp, q_all), 1) // n_ex
    t_of = lax.broadcasted_iota(jnp.int32, (q_all, n_tok), 1).astype(jnp.float32)

    def score(first, wait_train):
        mine = row_of == core * n_blocks + first + block_of
        stop = jnp.sum(jnp.where(mine, stops, 0.0), axis=0, keepdims=True)
        start = jnp.sum(jnp.where(mine, starts, 0.0), axis=0, keepdims=True)
        stop = jnp.broadcast_to(stop, (n_tok, q_all)).T
        start = jnp.broadcast_to(start, (n_tok, q_all)).T
        member = jnp.where((t_of >= start) & (t_of < stop), 1.0, 0.0).astype(jnp.bfloat16)
        gap = jnp.zeros((n_tok, K), jnp.bfloat16)

        for j in range(group):
            at = first + j

            @pl.when(jnp.logical_not(owner & (at == slot)))
            def _():
                for p in range(2):
                    pltpu.make_async_remote_copy(
                        xg.at[at, p], xg.at[at, p], b_send.at[p, 0], b_recv.at[at, p],
                        **peer(tensor=sibling)).wait_recv()

            x = xg[at, 0].astype(jnp.float32)
            g = xg[at, 1].astype(jnp.float32).T.astype(jnp.bfloat16)
            own = member[j * n_ex:(j + 1) * n_ex]
            for i in range(K):
                row = jnp.broadcast_to(x[i:i + 1], (16, n_tok)).astype(jnp.bfloat16)
                row = jnp.concatenate([row] * (n_ex // 16), axis=0)
                outer[i // 2 * n_ex:(i // 2 + 1) * n_ex, i % 2 * n_tok:(i % 2 + 1) * n_tok] = row * own
            pair = jnp.concatenate(
                [jnp.concatenate([g, gap], axis=1), jnp.concatenate([gap, g], axis=1)], axis=0)
            f = nn(outer[...], pair).astype(jnp.bfloat16)
            for i in range(K // 2):
                feats[j * n_ex:(j + 1) * n_ex, i * 2 * K:(i + 1) * 2 * K] = f[i * n_ex:(i + 1) * n_ex]

        wait_train()
        half = K * K // 2
        acc = nt(train[0], feats[:, :half]) + nt(train[1], feats[:, half:])
        return acc.T.astype(out_ref.dtype)

    def train_here():
        own_train.wait()
        pltpu.make_async_remote_copy(
            train_hbm, train.at[sibling], swap_send, swap_recv, **peer(tensor=sibling)).wait_recv()

    if n_blocks == group:
        out_ref[...] = score(0, train_here)
    else:
        train_here()

        def step(s, carry):
            out_ref[pl.ds(pl.multiple_of(s * q_all, q_all), q_all), :] = score(s * group, lambda: None)
            return carry

        lax.fori_loop(0, n_blocks // group, step, 0)

    swap.wait_send()

    @pl.when(jnp.logical_not(owner))
    def _():
        for p in range(2):
            to_owner(p).wait_send()

    @pl.when(owner)
    def _():
        for p in range(2):
            each_peer(lambda k: to_peer(p, k).wait_send())


def shards(n_dp, tokens_in, grads_out, proj_in, proj_out, lengths, train_feats):
    n_tok, d = tokens_in.shape
    ff = grads_out.shape[1]
    K = proj_in.shape[1]
    n_ex = lengths.shape[1]
    n_train, half = train_feats.shape
    n_blocks = n_dp // 2
    group = min(GROUP, n_blocks)
    bf16, f32 = jnp.bfloat16, jnp.float32
    dma = pltpu.SemaphoreType.DMA
    return pl.pallas_call(
        functools.partial(kernel, n_dp),
        out_shape=jax.ShapeDtypeStruct((n_blocks * n_ex, n_train), bf16),
        in_specs=[pl.BlockSpec(memory_space=pltpu.HBM)] * 6,
        out_specs=pl.BlockSpec(memory_space=pltpu.VMEM),
        scratch_shapes=[
            pltpu.VMEM((n_tok, d), bf16),
            pltpu.VMEM((n_tok, ff), bf16),
            pltpu.VMEM((K, d), bf16),
            pltpu.VMEM((K, ff), bf16),
            pltpu.VMEM(lengths.shape, jnp.int32),
            pltpu.VMEM((2, n_train, half), bf16),
            pltpu.VMEM((2, K, n_tok), f32),
            pltpu.VMEM((2, K, n_tok), f32),
            pltpu.VMEM((n_blocks, 2, K, n_tok), bf16),
            pltpu.VMEM((K // 2 * n_ex, 2 * n_tok), bf16),
            pltpu.VMEM((group * n_ex, K * K), bf16),
            dma((3 + 2 * G_PIECES,)),
            dma,
            dma,
            dma,
            dma((2,)),
            dma((2,)),
            dma((2, n_dp)),
            dma((n_blocks, 2)),
        ],
        compiler_params=pltpu.CompilerParams(
            collective_id=0, has_side_effects=True, vmem_limit_bytes=40 * 1024 * 1024),
        cost_estimate=pl.CostEstimate(flops=10**9, bytes_accessed=5 * 10**6, transcendentals=0),
    )(*[pltpu.with_memory_space_constraint(a, pltpu.HBM) for a in (tokens_in, grads_out, proj_in.T, proj_out.T, lengths, train_feats)])


def solution(mesh):
    return jax.shard_map(
        functools.partial(shards, mesh.shape["dp"]),
        mesh=mesh,
        in_specs=(
            P(("groups", "dp"), "tensor"),
            P(("groups", "dp"), "tensor"),
            P("tensor", None),
            P("tensor", None),
            P("groups", None),
            P(("groups", "dp"), "tensor"),
        ),
        out_specs=P(("groups", "tensor"), "dp"),
        check_vma=False,
    )
```

```python
import functools

import jax
import jax.numpy as jnp
from jax import lax
from jax.experimental import pallas as pl
from jax.experimental.pallas import tpu as pltpu
from jax.sharding import PartitionSpec as P

G_PIECES = 2
GROUP = 4


ORDERS = [4, 0, 2, 6, 3, 5, 1, 7], [0, 1, 2, 3, 4, 5, 6, 7]


def peer(**axes):
    return dict(device_id=axes, device_id_type=pl.DeviceIdType.MESH)


def nt(a, b):
    return lax.dot_general(a, b, (((1,), (1,)), ((), ())), preferred_element_type=jnp.float32)


def nn(a, b):
    return jnp.dot(a, b, preferred_element_type=jnp.float32)


def kernel(n_dp, tok_hbm, grd_hbm, pin_hbm, pout_hbm, len_hbm, train_hbm, out_ref,
           tok, grd, pin, pout, lens, train, part, other, xg, outer, member_ref, feats,
           load_sem, train_sem, swap_send, swap_recv, a_send, a_recv, b_send, b_recv):
    n_blocks = n_dp // 2
    group = min(GROUP, n_blocks)
    dp = lax.axis_index("dp")
    core = lax.axis_index("tensor")
    sibling = 1 - core
    owner = dp // n_blocks == core
    slot = lax.rem(dp, n_blocks)
    K, n_tok = part.shape[1:]
    n_ex = lens.shape[1]
    ff = grd.shape[1] // G_PIECES

    barrier = pltpu.get_barrier_semaphore()
    pl.semaphore_signal(barrier, inc=1, **peer(tensor=sibling))

    def greet(j, carry):
        to = core * n_blocks + j

        @pl.when(to != dp)
        def _():
            pl.semaphore_signal(barrier, inc=1, **peer(dp=to))

        return carry

    lax.fori_loop(0, n_blocks, greet, 0, unroll=n_blocks <= 8)

    loads = [
        pltpu.make_async_copy(pin_hbm, pin, load_sem.at[0]),
        pltpu.make_async_copy(tok_hbm, tok, load_sem.at[1]),
    ]
    for k in range(G_PIECES):
        cols = pl.ds(k * ff, ff)
        loads.append(pltpu.make_async_copy(pout_hbm.at[:, cols], pout.at[:, cols], load_sem.at[2 + 2 * k]))
        loads.append(pltpu.make_async_copy(grd_hbm.at[:, cols], grd.at[:, cols], load_sem.at[3 + 2 * k]))
    loads.append(pltpu.make_async_copy(len_hbm, lens, load_sem.at[2 + 2 * G_PIECES]))
    for load in loads:
        load.start()
    own_train = pltpu.make_async_copy(train_hbm, train.at[core], train_sem)

    swap = pltpu.make_async_remote_copy(
        train_hbm, train.at[core], swap_send, swap_recv, **peer(tensor=sibling))

    def to_owner(p):
        return pltpu.make_async_remote_copy(
            part.at[p], other.at[p], a_send.at[p], a_recv.at[p], **peer(tensor=sibling))

    def each_peer(act):
        def one(t):
            @pl.when(t != dp)
            def _():
                act(pltpu.make_async_remote_copy(
                    xg.at[slot], xg.at[slot], b_send.at[t], b_recv.at[slot], **peer(dp=t)))

        if n_dp == len(ORDERS[0]):
            for low, high in zip(*ORDERS):
                one(jnp.where(core == 0, low, high))
        else:
            def step(t, carry):
                one(t)
                return carry

            lax.fori_loop(0, n_dp, step, 0)

    def hand_over(p):
        @pl.when(jnp.logical_not(owner))
        def _():
            if p == 0:
                pl.semaphore_wait(barrier, 1)
            to_owner(p).start()

    def spread():
        @pl.when(owner)
        def _():
            for p in range(2):
                to_owner(p).wait_recv()
                xg[slot, p] = (part[p] + other[p]).astype(jnp.bfloat16)
            pl.semaphore_wait(barrier, n_dp)
            each_peer(lambda copy: copy.start())

    loads[0].wait()
    loads[1].wait()
    part[0] = nt(pin[...], tok[...])
    hand_over(0)
    for k in range(G_PIECES):
        loads[2 + 2 * k].wait()
        loads[3 + 2 * k].wait()
        term = nt(pout[:, k * ff:(k + 1) * ff], grd[:, k * ff:(k + 1) * ff])
        if k == 0:
            part[1] = term
        else:
            part[1] += term
    hand_over(1)
    spread()
    own_train.start()
    swap.start()

    loads[-1].wait()
    q_all = group * n_ex
    k_of = lax.broadcasted_iota(jnp.int32, (n_ex, q_all), 0)
    e_of = lax.rem(lax.broadcasted_iota(jnp.int32, (n_ex, q_all), 1), n_ex)
    lens_f = lens[...].astype(jnp.float32).astype(jnp.bfloat16)
    stops = nn(lens_f, (k_of <= e_of).astype(jnp.float32).astype(jnp.bfloat16))
    starts = nn(lens_f, (k_of < e_of).astype(jnp.float32).astype(jnp.bfloat16))
    row_of = lax.broadcasted_iota(jnp.int32, (n_dp, q_all), 0)
    block_of = lax.broadcasted_iota(jnp.int32, (n_dp, q_all), 1) // n_ex
    t_of = lax.broadcasted_iota(jnp.int32, (q_all, n_tok), 1).astype(jnp.float32)

    def score(first, wait_train):
        mine = row_of == core * n_blocks + first + block_of
        stop = jnp.sum(jnp.where(mine, stops, 0.0), axis=0, keepdims=True)
        start = jnp.sum(jnp.where(mine, starts, 0.0), axis=0, keepdims=True)
        stop = jnp.broadcast_to(stop, (n_tok, q_all)).T
        start = jnp.broadcast_to(start, (n_tok, q_all)).T
        member = jnp.where((t_of >= start) & (t_of < stop), 1.0, 0.0).astype(jnp.bfloat16)
        gap = jnp.zeros((K, n_tok), jnp.bfloat16)
        member_ref[...] = member

        def arrive(at):
            @pl.when(jnp.logical_not(owner & (at == slot)))
            def _():
                pltpu.make_async_remote_copy(
                    xg.at[at], xg.at[at], b_send.at[0], b_recv.at[at], **peer(tensor=sibling)).wait_recv()

        def fill(j, buffer):
            x = xg[first + j, 0].astype(jnp.float32)
            g = xg[first + j, 1]
            rows = pl.ds(pl.multiple_of(j * n_ex, n_ex), n_ex)
            own = member_ref[rows, :]
            for i in range(K):
                row = jnp.broadcast_to(x[i:i + 1], (16, n_tok)).astype(jnp.bfloat16)
                row = jnp.concatenate([row] * (n_ex // 16), axis=0)
                outer[buffer, i // 2 * n_ex:(i // 2 + 1) * n_ex, i % 2 * n_tok:(i % 2 + 1) * n_tok] = row * own
            pair = jnp.concatenate(
                [jnp.concatenate([g, gap], axis=1), jnp.concatenate([gap, g], axis=1)], axis=0)
            f = nt(outer[buffer], pair).astype(jnp.bfloat16)
            for i in range(K // 2):
                feats[rows, i * 2 * K:(i + 1) * 2 * K] = f[i * n_ex:(i + 1) * n_ex]

        for j in range(0, group, 2):
            turn = [j + k for k in range(min(2, group - j))]
            for at in turn:
                arrive(first + at)
            for k, at in enumerate(turn):
                fill(at, k)

        wait_train()
        half = K * K // 2
        terms = []
        rows = train.shape[1] // 3
        for r in range(3):
            acc = nt(feats[:, :half], train[0, r * rows:(r + 1) * rows]) + nt(feats[:, half:], train[1, r * rows:(r + 1) * rows])
            terms.append(acc.astype(out_ref.dtype))
        return jnp.concatenate(terms, axis=1)

    def train_here():
        own_train.wait()
        pltpu.make_async_remote_copy(
            train_hbm, train.at[sibling], swap_send, swap_recv, **peer(tensor=sibling)).wait_recv()

    if n_blocks == group:
        out_ref[...] = score(0, train_here)
    else:
        train_here()

        def step(s, carry):
            out_ref[pl.ds(pl.multiple_of(s * q_all, q_all), q_all), :] = score(s * group, lambda: None)
            return carry

        lax.fori_loop(0, n_blocks // group, step, 0)

    swap.wait_send()

    @pl.when(jnp.logical_not(owner))
    def _():
        for p in range(2):
            to_owner(p).wait_send()

    @pl.when(owner)
    def _():
        each_peer(lambda copy: copy.wait_send())


def shards(n_dp, tokens_in, grads_out, proj_in, proj_out, lengths, train_feats):
    n_tok, d = tokens_in.shape
    ff = grads_out.shape[1]
    K = proj_in.shape[1]
    n_ex = lengths.shape[1]
    n_train, half = train_feats.shape
    n_blocks = n_dp // 2
    group = min(GROUP, n_blocks)
    bf16, f32 = jnp.bfloat16, jnp.float32
    dma = pltpu.SemaphoreType.DMA
    return pl.pallas_call(
        functools.partial(kernel, n_dp),
        out_shape=jax.ShapeDtypeStruct((n_blocks * n_ex, n_train), bf16),
        in_specs=[pl.BlockSpec(memory_space=pltpu.HBM)] * 6,
        out_specs=pl.BlockSpec(memory_space=pltpu.VMEM),
        scratch_shapes=[
            pltpu.VMEM((n_tok, d), bf16),
            pltpu.VMEM((n_tok, ff), bf16),
            pltpu.VMEM((K, d), bf16),
            pltpu.VMEM((K, ff), bf16),
            pltpu.VMEM(lengths.shape, jnp.int32),
            pltpu.VMEM((2, n_train, half), bf16),
            pltpu.VMEM((2, K, n_tok), f32),
            pltpu.VMEM((2, K, n_tok), f32),
            pltpu.VMEM((n_blocks, 2, K, n_tok), bf16),
            pltpu.VMEM((2, K // 2 * n_ex, 2 * n_tok), bf16),
            pltpu.VMEM((group * n_ex, n_tok), bf16),
            pltpu.VMEM((group * n_ex, K * K), bf16),
            dma((3 + 2 * G_PIECES,)),
            dma,
            dma,
            dma,
            dma((2,)),
            dma((2,)),
            dma((n_dp,)),
            dma((n_blocks,)),
        ],
        compiler_params=pltpu.CompilerParams(
            collective_id=0, has_side_effects=True, vmem_limit_bytes=40 * 1024 * 1024),
        cost_estimate=pl.CostEstimate(flops=10**9, bytes_accessed=5 * 10**6, transcendentals=0),
    )(*[pltpu.with_memory_space_constraint(a, pltpu.HBM) for a in (tokens_in, grads_out, proj_in.T, proj_out.T, lengths, train_feats)])


def solution(mesh):
    return jax.shard_map(
        functools.partial(shards, mesh.shape["dp"]),
        mesh=mesh,
        in_specs=(
            P(("groups", "dp"), "tensor"),
            P(("groups", "dp"), "tensor"),
            P("tensor", None),
            P("tensor", None),
            P("groups", None),
            P(("groups", "dp"), "tensor"),
        ),
        out_specs=P(("groups", "tensor"), "dp"),
        check_vma=False,
    )
```

```python
import functools

import jax
import jax.numpy as jnp
from jax import lax
from jax.experimental import pallas as pl
from jax.experimental.pallas import tpu as pltpu
from jax.sharding import PartitionSpec as P

G_PIECES = 2
GROUP = 4


ORDERS = [4, 0, 2, 6, 3, 5, 1, 7], [0, 2, 1, 3, 4, 5, 6, 7]


def peer(**axes):
    return dict(device_id=axes, device_id_type=pl.DeviceIdType.MESH)


def nt(a, b):
    return lax.dot_general(a, b, (((1,), (1,)), ((), ())), preferred_element_type=jnp.float32)


def nn(a, b):
    return jnp.dot(a, b, preferred_element_type=jnp.float32)


def kernel(n_dp, tok_hbm, grd_hbm, pin_hbm, pout_hbm, len_hbm, train_hbm, out_ref,
           tok, grd, pin, pout, lens, train, part, other, xg, mine, halves, outer, member_ref, feats,
           load_sem, train_sem, swap_send, swap_recv, a_send, a_recv, b_send, b_recv, half_send, half_recv):
    n_blocks = n_dp // 2
    group = min(GROUP, n_blocks)
    dp = lax.axis_index("dp")
    core = lax.axis_index("tensor")
    sibling = 1 - core
    owner = dp // n_blocks == core
    slot = lax.rem(dp, n_blocks)
    top = dp >= n_dp - 2
    whole = (dp == 0) & (core == 1)
    K, n_tok = part.shape[1:]
    n_ex = lens.shape[1]
    ff = grd.shape[1] // G_PIECES

    barrier = pltpu.get_barrier_semaphore()
    pl.semaphore_signal(barrier, inc=1, **peer(tensor=sibling))

    def greet(j, carry):
        to = core * n_blocks + j

        @pl.when(to != dp)
        def _():
            pl.semaphore_signal(barrier, inc=1, **peer(dp=to))

        return carry

    lax.fori_loop(0, n_blocks, greet, 0, unroll=n_blocks <= 8)

    @pl.when(whole)
    def _():
        for k in range(2):
            pl.semaphore_signal(barrier, inc=1, **peer(dp=n_dp - 2 + k, tensor=0))

    loads = [
        pltpu.make_async_copy(pin_hbm, pin, load_sem.at[0]),
        pltpu.make_async_copy(tok_hbm, tok, load_sem.at[1]),
    ]
    for k in range(G_PIECES):
        cols = pl.ds(k * ff, ff)
        loads.append(pltpu.make_async_copy(pout_hbm.at[:, cols], pout.at[:, cols], load_sem.at[2 + 2 * k]))
        loads.append(pltpu.make_async_copy(grd_hbm.at[:, cols], grd.at[:, cols], load_sem.at[3 + 2 * k]))
    loads.append(pltpu.make_async_copy(len_hbm, lens, load_sem.at[2 + 2 * G_PIECES]))
    for load in loads:
        load.start()
    own_train = pltpu.make_async_copy(train_hbm, train.at[core], train_sem)

    swap = pltpu.make_async_remote_copy(
        train_hbm, train.at[core], swap_send, swap_recv, **peer(tensor=sibling))

    def to_owner(p):
        return pltpu.make_async_remote_copy(
            part.at[p], other.at[p], a_send.at[p], a_recv.at[p], **peer(tensor=sibling))

    def each_peer(act):
        def one(t):
            @pl.when((t != dp) & jnp.logical_not((core == 1) & top & (t == 0)))
            def _():
                act(pltpu.make_async_remote_copy(
                    xg.at[slot], xg.at[slot], b_send.at[t], b_recv.at[slot], **peer(dp=t)))

        if n_dp == len(ORDERS[0]):
            for low, high in zip(*ORDERS):
                one(jnp.where(core == 0, low, high))
        else:
            def step(t, carry):
                one(t)
                return carry

            lax.fori_loop(0, n_dp, step, 0)

    def to_whole():
        place = lax.rem(dp, 2)
        return pltpu.make_async_remote_copy(
            mine, halves.at[place, core], half_send, half_recv.at[place, core], **peer(dp=0, tensor=1))

    def hand_half():
        @pl.when(top)
        def _():
            mine[...] = part[...].astype(jnp.bfloat16)
            to_whole().start()

    def hand_over(p):
        @pl.when(jnp.logical_not(owner))
        def _():
            if p == 0:
                pl.semaphore_wait(barrier, 1 + top.astype(jnp.int32))
            to_owner(p).start()

    def spread():
        @pl.when(owner)
        def _():
            pl.semaphore_wait(barrier, n_dp)
            hand_half()
            for p in range(2):
                to_owner(p).wait_recv()
                xg[slot, p] = (part[p] + other[p]).astype(jnp.bfloat16)
            each_peer(lambda copy: copy.start())

    loads[0].wait()
    loads[1].wait()
    part[0] = nt(pin[...], tok[...])
    hand_over(0)
    for k in range(G_PIECES):
        loads[2 + 2 * k].wait()
        loads[3 + 2 * k].wait()
        term = nt(pout[:, k * ff:(k + 1) * ff], grd[:, k * ff:(k + 1) * ff])
        if k == 0:
            part[1] = term
        else:
            part[1] += term
    hand_over(1)
    spread()

    @pl.when(jnp.logical_not(owner))
    def _():
        hand_half()

    own_train.start()
    swap.start()

    loads[-1].wait()
    q_all = group * n_ex
    k_of = lax.broadcasted_iota(jnp.int32, (n_ex, q_all), 0)
    e_of = lax.rem(lax.broadcasted_iota(jnp.int32, (n_ex, q_all), 1), n_ex)
    lens_f = lens[...].astype(jnp.float32).astype(jnp.bfloat16)
    stops = nn(lens_f, (k_of <= e_of).astype(jnp.float32).astype(jnp.bfloat16))
    starts = nn(lens_f, (k_of < e_of).astype(jnp.float32).astype(jnp.bfloat16))
    row_of = lax.broadcasted_iota(jnp.int32, (n_dp, q_all), 0)
    block_of = lax.broadcasted_iota(jnp.int32, (n_dp, q_all), 1) // n_ex
    t_of = lax.broadcasted_iota(jnp.int32, (q_all, n_tok), 1).astype(jnp.float32)

    def score(first, wait_train):
        mine = row_of == core * n_blocks + first + block_of
        stop = jnp.sum(jnp.where(mine, stops, 0.0), axis=0, keepdims=True)
        start = jnp.sum(jnp.where(mine, starts, 0.0), axis=0, keepdims=True)
        stop = jnp.broadcast_to(stop, (n_tok, q_all)).T
        start = jnp.broadcast_to(start, (n_tok, q_all)).T
        member = jnp.where((t_of >= start) & (t_of < stop), 1.0, 0.0).astype(jnp.bfloat16)
        gap = jnp.zeros((K, n_tok), jnp.bfloat16)
        member_ref[...] = member

        def arrive(at):
            split = whole & (at >= n_blocks - 2)

            @pl.when(split)
            def _():
                place = lax.rem(at, 2)
                for k in range(2):
                    pltpu.make_async_remote_copy(
                        halves.at[place, k], halves.at[place, k], half_send, half_recv.at[place, k],
                        **peer(tensor=sibling)).wait_recv()
                total = halves[place, 0].astype(jnp.float32) + halves[place, 1].astype(jnp.float32)
                xg[at] = total.astype(jnp.bfloat16)

            @pl.when(jnp.logical_not(split | (owner & (at == slot))))
            def _():
                pltpu.make_async_remote_copy(
                    xg.at[at], xg.at[at], b_send.at[0], b_recv.at[at], **peer(tensor=sibling)).wait_recv()

        def fill(j, buffer):
            x = xg[first + j, 0].astype(jnp.float32)
            g = xg[first + j, 1]
            rows = pl.ds(pl.multiple_of(j * n_ex, n_ex), n_ex)
            own = member_ref[rows, :]
            for i in range(K):
                row = jnp.broadcast_to(x[i:i + 1], (16, n_tok)).astype(jnp.bfloat16)
                row = jnp.concatenate([row] * (n_ex // 16), axis=0)
                outer[buffer, i // 2 * n_ex:(i // 2 + 1) * n_ex, i % 2 * n_tok:(i % 2 + 1) * n_tok] = row * own
            pair = jnp.concatenate(
                [jnp.concatenate([g, gap], axis=1), jnp.concatenate([gap, g], axis=1)], axis=0)
            f = nt(outer[buffer], pair).astype(jnp.bfloat16)
            for i in range(K // 2):
                feats[rows, i * 2 * K:(i + 1) * 2 * K] = f[i * n_ex:(i + 1) * n_ex]

        for j in range(0, group, 2):
            turn = [j + k for k in range(min(2, group - j))]
            for at in turn:
                arrive(first + at)
            for k, at in enumerate(turn):
                fill(at, k)

        wait_train()
        half = K * K // 2
        terms = []
        rows = train.shape[1] // 3
        for r in range(3):
            acc = nt(feats[:, :half], train[0, r * rows:(r + 1) * rows]) + nt(feats[:, half:], train[1, r * rows:(r + 1) * rows])
            terms.append(acc.astype(out_ref.dtype))
        return jnp.concatenate(terms, axis=1)

    def train_here():
        own_train.wait()
        pltpu.make_async_remote_copy(
            train_hbm, train.at[sibling], swap_send, swap_recv, **peer(tensor=sibling)).wait_recv()

    if n_blocks == group:
        out_ref[...] = score(0, train_here)
    else:
        train_here()

        def step(s, carry):
            out_ref[pl.ds(pl.multiple_of(s * q_all, q_all), q_all), :] = score(s * group, lambda: None)
            return carry

        lax.fori_loop(0, n_blocks // group, step, 0)

    swap.wait_send()

    @pl.when(top)
    def _():
        to_whole().wait_send()

    @pl.when(jnp.logical_not(owner))
    def _():
        for p in range(2):
            to_owner(p).wait_send()

    @pl.when(owner)
    def _():
        each_peer(lambda copy: copy.wait_send())


def shards(n_dp, tokens_in, grads_out, proj_in, proj_out, lengths, train_feats):
    n_tok, d = tokens_in.shape
    ff = grads_out.shape[1]
    K = proj_in.shape[1]
    n_ex = lengths.shape[1]
    n_train, half = train_feats.shape
    n_blocks = n_dp // 2
    group = min(GROUP, n_blocks)
    bf16, f32 = jnp.bfloat16, jnp.float32
    dma = pltpu.SemaphoreType.DMA
    return pl.pallas_call(
        functools.partial(kernel, n_dp),
        out_shape=jax.ShapeDtypeStruct((n_blocks * n_ex, n_train), bf16),
        in_specs=[pl.BlockSpec(memory_space=pltpu.HBM)] * 6,
        out_specs=pl.BlockSpec(memory_space=pltpu.VMEM),
        scratch_shapes=[
            pltpu.VMEM((n_tok, d), bf16),
            pltpu.VMEM((n_tok, ff), bf16),
            pltpu.VMEM((K, d), bf16),
            pltpu.VMEM((K, ff), bf16),
            pltpu.VMEM(lengths.shape, jnp.int32),
            pltpu.VMEM((2, n_train, half), bf16),
            pltpu.VMEM((2, K, n_tok), f32),
            pltpu.VMEM((2, K, n_tok), f32),
            pltpu.VMEM((n_blocks, 2, K, n_tok), bf16),
            pltpu.VMEM((2, K, n_tok), bf16),
            pltpu.VMEM((2, 2, 2, K, n_tok), bf16),
            pltpu.VMEM((2, K // 2 * n_ex, 2 * n_tok), bf16),
            pltpu.VMEM((group * n_ex, n_tok), bf16),
            pltpu.VMEM((group * n_ex, K * K), bf16),
            dma((3 + 2 * G_PIECES,)),
            dma,
            dma,
            dma,
            dma((2,)),
            dma((2,)),
            dma((n_dp,)),
            dma((n_blocks,)),
            dma,
            dma((2, 2)),
        ],
        compiler_params=pltpu.CompilerParams(
            collective_id=0, has_side_effects=True, vmem_limit_bytes=40 * 1024 * 1024),
        cost_estimate=pl.CostEstimate(flops=10**9, bytes_accessed=5 * 10**6, transcendentals=0),
    )(*[pltpu.with_memory_space_constraint(a, pltpu.HBM) for a in (tokens_in, grads_out, proj_in.T, proj_out.T, lengths, train_feats)])


def solution(mesh):
    return jax.shard_map(
        functools.partial(shards, mesh.shape["dp"]),
        mesh=mesh,
        in_specs=(
            P(("groups", "dp"), "tensor"),
            P(("groups", "dp"), "tensor"),
            P("tensor", None),
            P("tensor", None),
            P("groups", None),
            P(("groups", "dp"), "tensor"),
        ),
        out_specs=P(("groups", "tensor"), "dp"),
        check_vma=False,
    )
```
